32 devices in a mesh: grp: 4 (over y, x), cell: 8 (over z, core).
Axes of the slice: x: 2, y: 2, z: 4, core: 2. Of those that a mesh axis runs over, the one named last changes fastest.
Arguments:
- fields: bfloat16 [512, 32, 8192], P('grp', None, 'cell'), may hold values from -6 to 6
- scales: float32 [512, 32, 64], P('grp', None, 'cell'), may hold values from 0.25 to 4
- pod_basis: bfloat16 [8192, 64], P('cell'), may hold values from -0.0625 to 0.0625
- param_order: int32 [30], replicated, may hold values from 0 to 29, each once
Outputs:
- sobol_maps: float32 [30, 8192], P(None, 'cell')
- total_map: float32 [8192], P('cell')
The draws below stay inside these ranges and needn't reach their ends.
Inputs may be any that keep to these rules, and one draw needn't show every extreme that they name: `param_order`: each parameter appears exactly once.
All inputs are finite; a program needn't handle non-finite values.
Results may differ from the reference program's by a relative error of at most 0.0003.
The reference program's roundings to bfloat16 on the way (of `dequant`) count: a program that leaves them out, or rounds other values in their place, can miss the bound.
Values sent between devices are 32-bit elements; how exact they have to be, the bound alone decides.
A program may use at most 128 MiB of HBM per device.

```python
import math
import jax
import jax.numpy as jnp
from jax import lax

MODES = 64
PARAMS = 30
BLOCK = 128
ROW_GRP = 128
CELL_DEV = 1024
SLOTS = 32
ROWS = 512
CELLS = 8192
N_GRP = 4
N_CELL = 8


def block_scale(own_key, shape, cuts, smallest, largest):
    def one(position, shards_of):
        draws = jax.random.uniform(jax.random.fold_in(jax.random.fold_in(own_key, 6), position), (shards_of,), jnp.float32, smallest / len(cuts), largest / len(cuts))
        return jnp.repeat(jnp.exp(draws), shape[position] // shards_of).reshape((-1,) + (1,) * (len(shape) - position - 1))

    factor_of = one(*cuts[0])
    for cut in cuts[1:]:
        factor_of = factor_of * one(*cut)
    return factor_of


def bell_draw(stream_key, dims, deviation, limit, split=(), kind=jnp.bfloat16):
    level = block_scale(stream_key, dims, split, -0.22, 0.18) if split else 1.0
    result = jax.random.normal(stream_key, dims, jnp.float32) * deviation * level
    return jnp.minimum(jnp.maximum(result, -limit), limit).astype(kind)


def setup_inputs(seed: int = 0) -> dict:
    splits = jax.random.split(jax.random.key(seed), 5)
    return {
        "fields": bell_draw(splits[0], (ROWS, SLOTS, CELLS), 1.0, 6.0, ((0, 4), (2, 8))),
        "scales": jnp.clip(jnp.exp(math.log(4.0) - 2.7725887 * jax.random.uniform(splits[1], (ROWS, SLOTS, CELLS // BLOCK), jnp.float32) ** block_scale(splits[1], (ROWS, SLOTS, CELLS // BLOCK), ((0, 4), (2, 8)), -0.2, 0.2)), 0.25, 4.0),
        "pod_basis": bell_draw(splits[2], (CELLS, MODES), CELLS ** -0.5, 0.0625, ((0, 8),)),
        "param_order": jax.random.permutation(splits[3], PARAMS).astype(jnp.int32),
    }


def project(piece, scale_piece, basis_piece):
    rows, slots, cells = piece.shape
    blocks = scale_piece.shape[2]
    dequant = (piece.astype(jnp.float32).reshape(rows, slots, blocks, cells // blocks) * scale_piece[..., None]).astype(jnp.bfloat16)
    flat = dequant.reshape(rows * slots, cells)
    return jnp.dot(flat, basis_piece, preferred_element_type=jnp.float32).reshape(rows, slots, basis_piece.shape[1])


def moments(coefficients):
    first = coefficients[:, 0]
    second_set = coefficients[:, 1]
    swapped = coefficients[:, 2:] - first[:, None, :]
    cross = jnp.einsum('rk,rpl->pkl', second_set, swapped, precision=lax.Precision.HIGHEST)
    squares = jnp.dot(first.T, first, precision=lax.Precision.HIGHEST) + jnp.dot(second_set.T, second_set, precision=lax.Precision.HIGHEST)
    column_sums = jnp.sum(first, axis=0) + jnp.sum(second_set, axis=0)
    return cross, squares, column_sums


def finish(cross, squares, column_sums, row_total, param_order, pod_basis, cell_total):
    count = param_order.shape[0]
    slot_cov = cross / row_total
    selector = (param_order[:, None] == jnp.arange(count).astype(jnp.int32)[None, :]).astype(jnp.float32)
    param_cov = jnp.einsum('sp,skl->pkl', selector, slot_cov, precision=lax.Precision.HIGHEST)
    average = column_sums / (2.0 * row_total)
    covariance = squares / (2.0 * row_total) - average[:, None] * average[None, :]
    stacked = jnp.concatenate([param_cov, covariance[None]], axis=0)
    phi = pod_basis.astype(jnp.float32)

    def one_map(matrix):
        return cell_total * jnp.sum(jnp.dot(phi, matrix, precision=lax.Precision.HIGHEST) * phi, axis=1)

    all_maps = lax.map(one_map, stacked)
    return all_maps[:-1], all_maps[-1]


def reference(fields, scales, pod_basis, param_order):
    row_total = ROW_GRP * N_GRP

    def add_shard(shard_index, total):
        first_cell = (shard_index * CELL_DEV).astype(jnp.int32)
        first_block = (shard_index * (CELL_DEV // BLOCK)).astype(jnp.int32)
        piece = lax.dynamic_slice_in_dim(fields, first_cell, CELL_DEV, 2)
        scale_piece = lax.dynamic_slice_in_dim(scales, first_block, CELL_DEV // BLOCK, 2)
        basis_piece = lax.dynamic_slice_in_dim(pod_basis, first_cell, CELL_DEV, 0)
        return total + project(piece, scale_piece, basis_piece)

    coefficients = lax.fori_loop(0, N_CELL, add_shard, jnp.zeros((row_total, SLOTS, MODES), jnp.float32))
    cross, squares, column_sums = moments(coefficients)
    return finish(cross, squares, column_sums, float(row_total), param_order, pod_basis, float(CELLS))
```

```python
import functools

import jax
import jax.numpy as jnp
from jax import lax
from jax.experimental import pallas as pl
from jax.experimental.pallas import tpu as pltpu
from jax.sharding import PartitionSpec as P

MESH = pl.DeviceIdType.MESH
F32, BF16 = jnp.float32, jnp.bfloat16
LANES = 128
STEP = 8


def loop(count, body):
    if count <= 8:
        for i in range(count):
            body(i)
    else:
        pl.loop(0, count)(body)


def split(x, axis):
    high = x.astype(BF16)
    low = (x - high.astype(F32)).astype(BF16)
    return jnp.concatenate([high, low], axis=axis)


def dot(a, b):
    return jnp.dot(a, b, preferred_element_type=F32)


def kernel(
    groups, cells_n, row_total, cell_total,
    fields_ref, scale_ref, basis_ref, order_ref, out_ref,
    field_buf, scale_buf, weight_buf, coef,
    ab_part, ab_recv, ab_full,
    moment, grp_recv, quarter, cell_recv, cov_full, map_recv,
    field_sem, ab_send, ab_sem, abf_send, abf_sem,
    grp_send, grp_sem, cov_send, cov_sem, covf_send, covf_sem, map_send, map_sem,
):
    rows = field_buf.shape[1]
    half = field_buf.shape[2]
    blocks = scale_ref.shape[1]
    modes = basis_ref.shape[0]
    steps = rows // STEP
    gme = lax.axis_index("grp")
    cme = lax.axis_index("cell")

    barrier = pltpu.get_barrier_semaphore()

    def greet_cell(c):
        @pl.when(c != cme)
        def _():
            pl.semaphore_signal(barrier, inc=1, device_id={"cell": c}, device_id_type=MESH)

    def greet_grp(g):
        @pl.when(g != gme)
        def _():
            pl.semaphore_signal(barrier, inc=1, device_id={"grp": g}, device_id_type=MESH)

    def field_copy(h, i):
        row = pl.multiple_of(i * STEP, STEP)
        return pltpu.make_async_copy(
            fields_ref.at[pl.ds(row, STEP), pl.ds(h * half, half), :],
            field_buf.at[h, pl.ds(row, STEP)],
            field_sem.at[h, i],
        )

    for h in range(2):
        pl.loop(0, steps)(lambda i, h=h: field_copy(h, i).start())
    loop(cells_n, greet_cell)
    loop(groups, greet_grp)

    phi_t = basis_ref[...]
    phi = phi_t.astype(F32)
    empty = jnp.zeros_like(phi)
    weight_buf[0] = jnp.concatenate([phi, empty], axis=0).T.astype(BF16)
    weight_buf[1] = jnp.concatenate([empty, phi], axis=0).T.astype(BF16)
    for b in range(blocks):
        scale_buf[b] = scale_ref[:, b, :]

    def project(h):
        @pl.loop(0, steps)
        def _(i):
            field_copy(h, i).wait()
            row = pl.multiple_of(i * STEP, STEP)
            turn = lax.rem(rows - row, rows)
            columns = []
            for b in range(blocks):
                scale = pltpu.roll(scale_buf[b, h * half:(h + 1) * half, :], turn, 1)
                pieces = []
                for r in range(STEP):
                    piece = field_buf[h, row + r, :, b * LANES:(b + 1) * LANES].astype(F32)
                    pieces.append((piece * scale[:, r:r + 1]).astype(BF16))
                columns.append(jnp.concatenate(pieces, axis=0))
            dequant = jnp.concatenate(columns, axis=1)
            result = dot(dequant, weight_buf[h]).reshape(STEP, half, LANES)
            if h == 0:
                coef[pl.ds(row, STEP)] = result
            else:
                coef[pl.ds(row, STEP)] += result

    project(0)

    first = coef[:, 0, :]
    second = coef[:, 1, :]
    both = first + pltpu.roll(second, modes, 1)
    owners = ab_part.shape[0]
    chunk = rows // owners
    ab_part[...] = both.reshape(owners, chunk, LANES)
    pl.semaphore_wait(barrier, cells_n - 1 + groups - 1)

    def ab_copy(owner, source):
        return pltpu.make_async_remote_copy(
            src_ref=ab_part.at[owner], dst_ref=ab_recv.at[source],
            send_sem=ab_send.at[owner], recv_sem=ab_sem.at[source],
            device_id={"cell": owner}, device_id_type=MESH,
        )

    def abf_copy(owner, target):
        return pltpu.make_async_remote_copy(
            src_ref=ab_full.at[owner], dst_ref=ab_full.at[owner],
            send_sem=abf_send.at[target], recv_sem=abf_sem.at[owner],
            device_id={"cell": target}, device_id_type=MESH,
        )

    def each(count, me, body):
        def guarded(c):
            @pl.when(c != me)
            def _():
                body(c)
        loop(count, guarded)

    each(owners, cme, lambda o: ab_copy(o, cme).start())

    def as_owner(count, body):
        if count == cells_n:
            body()
        else:
            pl.when(cme < count)(body)

    @functools.partial(as_owner, owners)
    def _():
        ab_full[cme] = ab_part[cme]

        def add(c):
            ab_copy(cme, c).wait_recv()
            ab_full[cme] += ab_recv[c]
        each(cells_n, cme, add)
        each(cells_n, cme, lambda c: abf_copy(cme, c).start())

    project(1)

    each(owners, cme, lambda o: abf_copy(o, cme).wait_recv())
    whole = ab_full[...].reshape(rows, LANES)
    whole_t = whole.T
    a_t, b_t = whole_t[:modes], whole_t[modes:]
    b_split = split(b_t, 0)
    b_left = jnp.concatenate([b_split, b_split], axis=1)
    a_split = split(a_t, 0)

    lane = lax.broadcasted_iota(jnp.int32, (rows, LANES), 1)
    part = ab_part[...].reshape(rows, LANES)
    swapped_part = pltpu.roll(part, modes, 1)
    a_twice = jnp.where(lane < modes, part, swapped_part)
    b_twice = jnp.where(lane < modes, swapped_part, part)
    a_right = jnp.where(lane < modes, 0.0, a_twice)

    sums = jnp.sum(part, axis=0, keepdims=True)
    sums = sums + pltpu.roll(sums, modes, 1)
    own_square = dot(jnp.concatenate([a_split, a_split], axis=1), split(a_twice, 0))
    own_square = own_square[:modes] + own_square[modes:]
    mode_lane = lax.broadcasted_iota(jnp.int32, (modes, LANES), 1)

    def grp_copy(target, source):
        return pltpu.make_async_remote_copy(
            src_ref=moment.at[target], dst_ref=grp_recv.at[source],
            send_sem=grp_send.at[target], recv_sem=grp_sem.at[source],
            device_id={"grp": target}, device_id_type=MESH,
        )

    pairs = half // groups
    tiles = modes // 8
    for g in range(groups):
        for p in range(0, pairs, 2):
            sides = []
            for s in (g * pairs + p, g * pairs + p + 1):
                sides.append(coef[:, s, :] - (a_right if s < 2 else a_twice))
            product = dot(b_left, split(jnp.concatenate(sides, axis=1), 0))
            product = product[:modes] + product[modes:]
            for q in range(2):
                s = g * pairs + p + q
                matrix = product[:, q * LANES:(q + 1) * LANES]
                if s == 0:
                    matrix = jnp.where(mode_lane < modes, sums, matrix)
                if s == 1:
                    matrix = jnp.where(mode_lane < modes, matrix + own_square, matrix)
                at = (p + q) * tiles
                moment[g, at:at + tiles] = matrix.reshape(tiles, 8, LANES)

        @pl.when(g != gme)
        def _():
            grp_copy(g, gme).start()

    grp_recv[gme] = moment[gme]
    each(groups, gme, lambda g: grp_copy(gme, g).wait_recv())
    total = grp_recv[0]
    for g in range(1, groups):
        total = total + grp_recv[g]
    quarter[...] = total

    cov_owners, share = cov_full.shape[0], cov_full.shape[1]

    def cov_copy(owner, source):
        return pltpu.make_async_remote_copy(
            src_ref=quarter.at[pl.ds(owner * share, share)], dst_ref=cell_recv.at[source],
            send_sem=cov_send.at[owner], recv_sem=cov_sem.at[source],
            device_id={"cell": owner}, device_id_type=MESH,
        )

    def covf_copy(owner, target):
        return pltpu.make_async_remote_copy(
            src_ref=cov_full.at[owner], dst_ref=cov_full.at[owner],
            send_sem=covf_send.at[target], recv_sem=covf_sem.at[owner],
            device_id={"cell": target}, device_id_type=MESH,
        )

    each(cov_owners, cme, lambda o: cov_copy(o, cme).start())

    @functools.partial(as_owner, cov_owners)
    def _():
        cov_full[cme] = quarter[pl.ds(cme * share, share)]

        def add(c):
            cov_copy(cme, c).wait_recv()
            cov_full[cme] += cell_recv[c]
        each(cells_n, cme, add)
        each(cells_n, cme, lambda c: covf_copy(cme, c).start())

    slots = 2 * half
    count = order_ref.shape[1]
    param = lax.broadcasted_iota(jnp.int32, (slots, count), 0)
    chosen = (order_ref[...] == param).astype(F32).astype(BF16)
    swap = lax.broadcasted_iota(jnp.int32, (count, slots), 0) + 2
    place = lax.broadcasted_iota(jnp.int32, (count, slots), 1)
    per = 2 * pairs
    stands = (lax.rem(place, per) // pairs) * half + (place // per) * pairs + lax.rem(place, pairs)
    select = dot(chosen, (stands == swap).astype(F32).astype(BF16))
    out_row = lax.broadcasted_iota(jnp.int32, (slots, slots), 0)
    in_row = lax.broadcasted_iota(jnp.int32, (slots, slots), 1)
    select = jnp.where((out_row == count) & (in_row == 1), 1.0, select).astype(BF16)
    select = jnp.concatenate([select] * 4, axis=1)
    basis_four = jnp.concatenate([phi_t] * 4, axis=0)

    each(cov_owners, cme, lambda o: covf_copy(o, cme).wait_recv())
    pair_rows = cov_full[...].reshape(pairs * modes, LANES)
    matrices = [pair_rows[p * modes:(p + 1) * modes] * (1.0 / row_total) for p in range(pairs)]
    average = matrices[0] * 0.5
    outer = average * jnp.pad(average.T[:modes], ((0, 0), (0, LANES - modes)))
    special = (mode_lane < modes) & (gme == 0)
    matrices[1] = jnp.where(special, matrices[1] * 0.5 - outer, matrices[1])
    left = jnp.concatenate(
        [jnp.where(mode_lane < modes, m, 0.0) for m in matrices]
        + [jnp.where(mode_lane < modes, 0.0, m) for m in matrices],
        axis=0,
    )
    products = dot(split(left, 1), basis_four)
    cells = products.shape[1]
    products = products.reshape(per, modes, cells) * phi[None]
    map_recv[gme] = jnp.sum(products, axis=1) * cell_total

    def map_copy(source, target):
        return pltpu.make_async_remote_copy(
            src_ref=map_recv.at[source], dst_ref=map_recv.at[source],
            send_sem=map_send.at[target], recv_sem=map_sem.at[source],
            device_id={"grp": target}, device_id_type=MESH,
        )

    each(groups, gme, lambda g: map_copy(gme, g).start())
    each(groups, gme, lambda g: map_copy(g, gme).wait_recv())
    maps = map_recv[...].reshape(slots, cells)
    high = maps.astype(BF16)
    rest = maps - high.astype(F32)
    middle = rest.astype(BF16)
    low = (rest - middle.astype(F32)).astype(BF16)
    parts = jnp.concatenate([high, middle, low, jnp.zeros_like(low)], axis=0)
    out_ref[...] = dot(select, parts)

    each(owners, cme, lambda o: ab_copy(o, cme).wait_send())
    each(groups, gme, lambda g: grp_copy(g, gme).wait_send())
    each(cov_owners, cme, lambda o: cov_copy(o, cme).wait_send())
    each(groups, gme, lambda g: map_copy(gme, g).wait_send())
    as_owner(owners, lambda: each(cells_n, cme, lambda c: abf_copy(cme, c).wait_send()))
    as_owner(cov_owners, lambda: each(cells_n, cme, lambda c: covf_copy(cme, c).wait_send()))


def on_device(fields, scales, pod_basis, param_order):
    groups = lax.axis_size("grp")
    cells_n = lax.axis_size("cell")
    rows, slots, cells = fields.shape
    blocks = scales.shape[2]
    modes = pod_basis.shape[1]
    half = slots // 2
    pairs = half // groups
    count = param_order.shape[0]
    owners = min(cells_n, rows // 8)
    tiles = pairs * modes // 8
    cov_owners = min(cells_n, tiles)
    share = tiles // cov_owners
    dma = pltpu.SemaphoreType.DMA
    vmem = pl.BlockSpec(memory_space=pltpu.VMEM)
    packed = pl.pallas_call(
        functools.partial(
            kernel, groups, cells_n, float(rows * groups), float(cells * cells_n)
        ),
        out_shape=jax.ShapeDtypeStruct((slots, cells), F32),
        in_specs=[pl.BlockSpec(memory_space=pl.ANY), vmem, vmem, vmem],
        out_specs=vmem,
        scratch_shapes=[
            pltpu.VMEM((2, rows, half, cells), BF16),
            pltpu.VMEM((blocks, slots, rows), F32),
            pltpu.VMEM((2, cells, LANES), BF16),
            pltpu.VMEM((rows, half, LANES), F32),
            pltpu.VMEM((owners, rows // owners, LANES), F32),
            pltpu.VMEM((cells_n, rows // owners, LANES), F32),
            pltpu.VMEM((owners, rows // owners, LANES), F32),
            pltpu.VMEM((groups, tiles, 8, LANES), F32),
            pltpu.VMEM((groups, tiles, 8, LANES), F32),
            pltpu.VMEM((tiles, 8, LANES), F32),
            pltpu.VMEM((cells_n, share, 8, LANES), F32),
            pltpu.VMEM((cov_owners, share, 8, LANES), F32),
            pltpu.VMEM((groups, 2 * pairs, cells), F32),
            dma((2, rows // STEP)),
            dma((owners,)), dma((cells_n,)), dma((cells_n,)), dma((owners,)),
            dma((groups,)), dma((groups,)),
            dma((cov_owners,)), dma((cells_n,)), dma((cells_n,)), dma((cov_owners,)),
            dma((groups,)), dma((groups,)),
        ],
        compiler_params=pltpu.CompilerParams(
            collective_id=0, has_side_effects=True, vmem_limit_bytes=40 * 2**20
        ),
        cost_estimate=pl.CostEstimate(
            flops=2 * rows * slots * cells * modes, bytes_accessed=2 * rows * slots * cells,
            transcendentals=0,
        ),
    )(
        fields,
        jnp.transpose(scales, (1, 2, 0)),
        jnp.transpose(pod_basis),
        param_order.reshape(1, count),
    )
    return packed[:count], packed[count]


def solution(mesh):
    placed = (P("grp", None, "cell"), P("grp", None, "cell"), P("cell", None), P())
    return jax.shard_map(
        on_device,
        mesh=mesh,
        in_specs=placed,
        out_specs=(P(None, "cell"), P("cell")),
        check_vma=False,
    )
```

```python
import functools

import jax
import jax.numpy as jnp
from jax import lax
from jax.experimental import pallas as pl
from jax.experimental.pallas import tpu as pltpu
from jax.sharding import PartitionSpec as P

MESH = pl.DeviceIdType.MESH
F32, BF16 = jnp.float32, jnp.bfloat16
LANES = 128
STEP = 16


def loop(count, body):
    if count <= 8:
        for i in range(count):
            body(i)
    else:
        pl.loop(0, count)(body)


def split(x, axis):
    high = x.astype(BF16)
    low = (x - high.astype(F32)).astype(BF16)
    return jnp.concatenate([high, low], axis=axis)


def dot(a, b):
    return jnp.dot(a, b, preferred_element_type=F32)


def kernel(
    groups, cells_n, row_total, cell_total,
    fields_ref, scale_any, basis_any, order_any, out_ref,
    scale_ref, basis_ref, order_ref, field_buf, scale_buf, weight_buf, coef,
    ab_part, ab_recv, ab_full,
    moment, grp_recv, quarter, cell_recv, cov_full, map_recv,
    input_sem, field_sem, ab_send, ab_sem, abf_send, abf_sem,
    grp_send, grp_sem, cov_send, cov_sem, covf_send, covf_sem, map_send, map_sem,
):
    rows = field_buf.shape[1]
    half = field_buf.shape[2]
    blocks = scale_ref.shape[1]
    modes = basis_ref.shape[0]
    steps = rows // STEP
    gme = lax.axis_index("grp")
    cme = lax.axis_index("cell")

    barrier = pltpu.get_barrier_semaphore()

    def greet_cell(c):
        @pl.when(c != cme)
        def _():
            pl.semaphore_signal(barrier, inc=1, device_id={"cell": c}, device_id_type=MESH)

    def greet_grp(g):
        @pl.when(g != gme)
        def _():
            pl.semaphore_signal(barrier, inc=1, device_id={"grp": g}, device_id_type=MESH)

    def field_copy(h, i):
        row = pl.multiple_of(i * STEP, STEP)
        return pltpu.make_async_copy(
            fields_ref.at[pl.ds(row, STEP), pl.ds(h * half, half), :],
            field_buf.at[h, pl.ds(row, STEP)],
            field_sem.at[h, i],
        )

    small = [
        pltpu.make_async_copy(source, kept, input_sem.at[n])
        for n, (source, kept) in enumerate(
            [(basis_any, basis_ref), (scale_any, scale_ref), (order_any, order_ref)]
        )
    ]
    for copy in small:
        copy.start()
    for h in range(2):
        pl.loop(0, steps)(lambda i, h=h: field_copy(h, i).start())
    loop(cells_n, greet_cell)
    loop(groups, greet_grp)

    small[0].wait()
    phi_t = basis_ref[...]
    phi = phi_t.astype(F32)
    empty = jnp.zeros_like(phi)
    weight_buf[0] = jnp.concatenate([phi, empty], axis=0).T.astype(BF16)
    weight_buf[1] = jnp.concatenate([empty, phi], axis=0).T.astype(BF16)
    small[1].wait()
    small[2].wait()
    for b in range(blocks):
        scale_buf[b] = scale_ref[:, b, :]

    def project(h, begin, end):
        @pl.loop(begin, end)
        def _(i):
            field_copy(h, i).wait()
            row = pl.multiple_of(i * STEP, STEP)
            turn = lax.rem(rows - row, rows)
            columns = []
            for b in range(blocks):
                scale = pltpu.roll(scale_buf[b, h * half:(h + 1) * half, :], turn, 1)
                pieces = []
                for r in range(STEP):
                    piece = field_buf[h, row + r, :, b * LANES:(b + 1) * LANES].astype(F32)
                    pieces.append((piece * scale[:, r:r + 1]).astype(BF16))
                columns.append(jnp.concatenate(pieces, axis=0))
            dequant = jnp.concatenate(columns, axis=1)
            result = dot(dequant, weight_buf[h]).reshape(STEP, half, LANES)
            if h == 0:
                coef[pl.ds(row, STEP)] = result
            else:
                coef[pl.ds(row, STEP)] += result

    project(0, 0, steps)

    first = coef[:, 0, :]
    second = coef[:, 1, :]
    both = first + pltpu.roll(second, modes, 1)
    owners = ab_part.shape[0]
    chunk = rows // owners
    ab_part[...] = both.reshape(owners, chunk, LANES)
    pl.semaphore_wait(barrier, cells_n - 1 + groups - 1)

    def ab_copy(owner, source):
        return pltpu.make_async_remote_copy(
            src_ref=ab_part.at[owner], dst_ref=ab_recv.at[source],
            send_sem=ab_send.at[owner], recv_sem=ab_sem.at[source],
            device_id={"cell": owner}, device_id_type=MESH,
        )

    def abf_copy(owner, target):
        return pltpu.make_async_remote_copy(
            src_ref=ab_full.at[owner], dst_ref=ab_full.at[owner],
            send_sem=abf_send.at[target], recv_sem=abf_sem.at[owner],
            device_id={"cell": target}, device_id_type=MESH,
        )

    def each(count, me, body):
        def guarded(c):
            @pl.when(c != me)
            def _():
                body(c)
        loop(count, guarded)

    each(owners, cme, lambda o: ab_copy(o, cme).start())

    def as_owner(count, body):
        if count == cells_n:
            body()
        else:
            pl.when(cme < count)(body)

    project(1, 0, steps // 2)

    @functools.partial(as_owner, owners)
    def _():
        ab_full[cme] = ab_part[cme]

        def add(c):
            ab_copy(cme, c).wait_recv()
            ab_full[cme] += ab_recv[c]
        each(cells_n, cme, add)
        each(cells_n, cme, lambda c: abf_copy(cme, c).start())

    project(1, steps // 2, steps)

    each(owners, cme, lambda o: abf_copy(o, cme).wait_recv())
    whole = ab_full[...].reshape(rows, LANES)
    whole_t = whole.T
    a_t, b_t = whole_t[:modes], whole_t[modes:]
    b_split = split(b_t, 0)
    b_left = jnp.concatenate([b_split, b_split], axis=1)
    a_split = split(a_t, 0)

    lane = lax.broadcasted_iota(jnp.int32, (rows, LANES), 1)
    part = ab_part[...].reshape(rows, LANES)
    swapped_part = pltpu.roll(part, modes, 1)
    a_twice = jnp.where(lane < modes, part, swapped_part)
    b_twice = jnp.where(lane < modes, swapped_part, part)
    a_right = jnp.where(lane < modes, 0.0, a_twice)

    sums = jnp.sum(part, axis=0, keepdims=True)
    sums = sums + pltpu.roll(sums, modes, 1)
    own_square = dot(jnp.concatenate([a_split, a_split], axis=1), split(a_twice, 0))
    own_square = own_square[:modes] + own_square[modes:]
    mode_lane = lax.broadcasted_iota(jnp.int32, (modes, LANES), 1)

    def grp_copy(target, source):
        return pltpu.make_async_remote_copy(
            src_ref=moment.at[target], dst_ref=grp_recv.at[source],
            send_sem=grp_send.at[target], recv_sem=grp_sem.at[source],
            device_id={"grp": target}, device_id_type=MESH,
        )

    pairs = half // groups
    tiles = modes // 8
    for g in range(groups):
        for p in range(0, pairs, 2):
            sides = []
            for s in (g * pairs + p, g * pairs + p + 1):
                sides.append(coef[:, s, :] - (a_right if s < 2 else a_twice))
            product = dot(b_left, split(jnp.concatenate(sides, axis=1), 0))
            product = product[:modes] + product[modes:]
            for q in range(2):
                s = g * pairs + p + q
                matrix = product[:, q * LANES:(q + 1) * LANES]
                if s == 0:
                    matrix = jnp.where(mode_lane < modes, sums, matrix)
                if s == 1:
                    matrix = jnp.where(mode_lane < modes, matrix + own_square, matrix)
                at = (p + q) * tiles
                moment[g, at:at + tiles] = matrix.reshape(tiles, 8, LANES)

        @pl.when(g != gme)
        def _():
            grp_copy(g, gme).start()

    grp_recv[gme] = moment[gme]
    each(groups, gme, lambda g: grp_copy(gme, g).wait_recv())
    total = grp_recv[0]
    for g in range(1, groups):
        total = total + grp_recv[g]
    quarter[...] = total

    cov_owners, share = cov_full.shape[0], cov_full.shape[1]

    def cov_copy(owner, source):
        return pltpu.make_async_remote_copy(
            src_ref=quarter.at[pl.ds(owner * share, share)], dst_ref=cell_recv.at[source],
            send_sem=cov_send.at[owner], recv_sem=cov_sem.at[source],
            device_id={"cell": owner}, device_id_type=MESH,
        )

    def covf_copy(owner, target):
        return pltpu.make_async_remote_copy(
            src_ref=cov_full.at[owner], dst_ref=cov_full.at[owner],
            send_sem=covf_send.at[target], recv_sem=covf_sem.at[owner],
            device_id={"cell": target}, device_id_type=MESH,
        )

    each(cov_owners, cme, lambda o: cov_copy(o, cme).start())

    @functools.partial(as_owner, cov_owners)
    def _():
        cov_full[cme] = quarter[pl.ds(cme * share, share)]

        def add(c):
            cov_copy(cme, c).wait_recv()
            cov_full[cme] += cell_recv[c]
        each(cells_n, cme, add)
        each(cells_n, cme, lambda c: covf_copy(cme, c).start())

    slots = 2 * half
    count = order_ref.shape[1]
    param = lax.broadcasted_iota(jnp.int32, (slots, count), 0)
    chosen = (order_ref[...] == param).astype(F32).astype(BF16)
    swap = lax.broadcasted_iota(jnp.int32, (count, slots), 0) + 2
    place = lax.broadcasted_iota(jnp.int32, (count, slots), 1)
    per = 2 * pairs
    stands = (lax.rem(place, per) // pairs) * half + (place // per) * pairs + lax.rem(place, pairs)
    select = dot(chosen, (stands == swap).astype(F32).astype(BF16))
    out_row = lax.broadcasted_iota(jnp.int32, (slots, slots), 0)
    in_row = lax.broadcasted_iota(jnp.int32, (slots, slots), 1)
    select = jnp.where((out_row == count) & (in_row == 1), 1.0, select).astype(BF16)
    select = jnp.concatenate([select] * 4, axis=1)
    basis_four = jnp.concatenate([phi_t] * 4, axis=0)

    each(cov_owners, cme, lambda o: covf_copy(o, cme).wait_recv())
    pair_rows = cov_full[...].reshape(pairs * modes, LANES)
    matrices = [pair_rows[p * modes:(p + 1) * modes] * (1.0 / row_total) for p in range(pairs)]
    average = matrices[0] * 0.5
    outer = average * jnp.pad(average.T[:modes], ((0, 0), (0, LANES - modes)))
    special = (mode_lane < modes) & (gme == 0)
    matrices[1] = jnp.where(special, matrices[1] * 0.5 - outer, matrices[1])
    left = jnp.concatenate(
        [jnp.where(mode_lane < modes, m, 0.0) for m in matrices]
        + [jnp.where(mode_lane < modes, 0.0, m) for m in matrices],
        axis=0,
    )
    products = dot(split(left, 1), basis_four)
    cells = products.shape[1]
    products = products.reshape(per, modes, cells) * phi[None]
    map_recv[gme] = jnp.sum(products, axis=1) * cell_total

    def map_copy(source, target):
        return pltpu.make_async_remote_copy(
            src_ref=map_recv.at[source], dst_ref=map_recv.at[source],
            send_sem=map_send.at[target], recv_sem=map_sem.at[source],
            device_id={"grp": target}, device_id_type=MESH,
        )

    each(groups, gme, lambda g: map_copy(gme, g).start())
    each(groups, gme, lambda g: map_copy(g, gme).wait_recv())
    maps = map_recv[...].reshape(slots, cells)
    high = maps.astype(BF16)
    rest = maps - high.astype(F32)
    middle = rest.astype(BF16)
    low = (rest - middle.astype(F32)).astype(BF16)
    parts = jnp.concatenate([high, middle, low, jnp.zeros_like(low)], axis=0)
    out_ref[...] = dot(select, parts)

    each(owners, cme, lambda o: ab_copy(o, cme).wait_send())
    each(groups, gme, lambda g: grp_copy(g, gme).wait_send())
    each(cov_owners, cme, lambda o: cov_copy(o, cme).wait_send())
    each(groups, gme, lambda g: map_copy(gme, g).wait_send())
    as_owner(owners, lambda: each(cells_n, cme, lambda c: abf_copy(cme, c).wait_send()))
    as_owner(cov_owners, lambda: each(cells_n, cme, lambda c: covf_copy(cme, c).wait_send()))


def on_device(fields, scales, pod_basis, param_order):
    groups = lax.axis_size("grp")
    cells_n = lax.axis_size("cell")
    rows, slots, cells = fields.shape
    blocks = scales.shape[2]
    modes = pod_basis.shape[1]
    half = slots // 2
    pairs = half // groups
    count = param_order.shape[0]
    owners = min(cells_n, rows // 8)
    tiles = pairs * modes // 8
    cov_owners = min(cells_n, tiles)
    share = tiles // cov_owners
    dma = pltpu.SemaphoreType.DMA
    anywhere = pl.BlockSpec(memory_space=pl.ANY)
    vmem = pl.BlockSpec(memory_space=pltpu.VMEM)
    packed = pl.pallas_call(
        functools.partial(
            kernel, groups, cells_n, float(rows * groups), float(cells * cells_n)
        ),
        out_shape=jax.ShapeDtypeStruct((slots, cells), F32),
        in_specs=[anywhere] * 4,
        out_specs=vmem,
        scratch_shapes=[
            pltpu.VMEM((slots, blocks, rows), F32),
            pltpu.VMEM((modes, cells), BF16),
            pltpu.VMEM((1, count), jnp.int32),
            pltpu.VMEM((2, rows, half, cells), BF16),
            pltpu.VMEM((blocks, slots, rows), F32),
            pltpu.VMEM((2, cells, LANES), BF16),
            pltpu.VMEM((rows, half, LANES), F32),
            pltpu.VMEM((owners, rows // owners, LANES), F32),
            pltpu.VMEM((cells_n, rows // owners, LANES), F32),
            pltpu.VMEM((owners, rows // owners, LANES), F32),
            pltpu.VMEM((groups, tiles, 8, LANES), F32),
            pltpu.VMEM((groups, tiles, 8, LANES), F32),
            pltpu.VMEM((tiles, 8, LANES), F32),
            pltpu.VMEM((cells_n, share, 8, LANES), F32),
            pltpu.VMEM((cov_owners, share, 8, LANES), F32),
            pltpu.VMEM((groups, 2 * pairs, cells), F32),
            dma((3,)), dma((2, rows // STEP)),
            dma((owners,)), dma((cells_n,)), dma((cells_n,)), dma((owners,)),
            dma((groups,)), dma((groups,)),
            dma((cov_owners,)), dma((cells_n,)), dma((cells_n,)), dma((cov_owners,)),
            dma((groups,)), dma((groups,)),
        ],
        compiler_params=pltpu.CompilerParams(
            collective_id=0, has_side_effects=True, vmem_limit_bytes=62 * 2**20
        ),
        cost_estimate=pl.CostEstimate(
            flops=2 * rows * slots * cells * modes, bytes_accessed=2 * rows * slots * cells,
            transcendentals=0,
        ),
    )(
        fields,
        jnp.transpose(scales, (1, 2, 0)),
        jnp.transpose(pod_basis),
        param_order.reshape(1, count),
    )
    return packed[:count], packed[count]


def solution(mesh):
    placed = (P("grp", None, "cell"), P("grp", None, "cell"), P("cell", None), P())
    return jax.shard_map(
        on_device,
        mesh=mesh,
        in_specs=placed,
        out_specs=(P(None, "cell"), P("cell")),
        check_vma=False,
    )
```

```python
import functools

import jax
import jax.numpy as jnp
from jax import lax
from jax.experimental import pallas as pl
from jax.experimental.pallas import tpu as pltpu
from jax.sharding import PartitionSpec as P

MESH = pl.DeviceIdType.MESH
F32, BF16 = jnp.float32, jnp.bfloat16
LANES = 128
STEP = 16


def loop(count, body):
    if count <= 8:
        for i in range(count):
            body(i)
    else:
        pl.loop(0, count)(body)


def split(x, axis):
    high = x.astype(BF16)
    low = (x - high.astype(F32)).astype(BF16)
    return jnp.concatenate([high, low], axis=axis)


def dot(a, b):
    return jnp.dot(a, b, preferred_element_type=F32)


def kernel(
    groups, cells_n, row_total, cell_total,
    fields_ref, scale_any, basis_any, order_any, out_ref,
    scale_ref, basis_ref, order_ref, field_buf, scale_buf, weight_buf, coef,
    ab_part, ab_recv, ab_full,
    moment, pair_recv, grp_recv, quarter, cell_recv, cov_full, map_recv,
    input_sem, field_sem, ab_send, ab_sem, abf_send, abf_sem,
    pair_send, pair_sem, grp_send, grp_sem, cov_send, cov_sem, covf_send, covf_sem, map_send, map_sem,
):
    rows = field_buf.shape[1]
    half = field_buf.shape[2]
    blocks = scale_ref.shape[1]
    modes = basis_ref.shape[0]
    steps = rows // STEP
    gme = lax.axis_index("grp")
    cme = lax.axis_index("cell")

    barrier = pltpu.get_barrier_semaphore()

    def greet_cell(c):
        @pl.when(c != cme)
        def _():
            pl.semaphore_signal(barrier, inc=1, device_id={"cell": c}, device_id_type=MESH)

    def greet_grp(g):
        @pl.when(g != gme)
        def _():
            pl.semaphore_signal(barrier, inc=1, device_id={"grp": g}, device_id_type=MESH)

    def field_copy(h, i):
        row = pl.multiple_of(i * STEP, STEP)
        return pltpu.make_async_copy(
            fields_ref.at[pl.ds(row, STEP), pl.ds(h * half, half), :],
            field_buf.at[h, pl.ds(row, STEP)],
            field_sem.at[h, i],
        )

    small = [
        pltpu.make_async_copy(source, kept, input_sem.at[n])
        for n, (source, kept) in enumerate(
            [(basis_any, basis_ref), (scale_any, scale_ref), (order_any, order_ref)]
        )
    ]
    for copy in small:
        copy.start()
    for h in range(2):
        pl.loop(0, steps)(lambda i, h=h: field_copy(h, i).start())
    loop(cells_n, greet_cell)
    loop(groups, greet_grp)

    small[0].wait()
    phi_t = basis_ref[...]
    phi = phi_t.astype(F32)
    empty = jnp.zeros_like(phi)
    weight_buf[0] = jnp.concatenate([phi, empty], axis=0).T.astype(BF16)
    weight_buf[1] = jnp.concatenate([empty, phi], axis=0).T.astype(BF16)
    small[1].wait()
    small[2].wait()
    for b in range(blocks):
        scale_buf[b] = scale_ref[:, b, :]

    def project(h, begin, end):
        @pl.loop(begin, end)
        def _(i):
            field_copy(h, i).wait()
            row = pl.multiple_of(i * STEP, STEP)
            turn = lax.rem(rows - row, rows)
            columns = []
            for b in range(blocks):
                scale = pltpu.roll(scale_buf[b, h * half:(h + 1) * half, :], turn, 1)
                pieces = []
                for r in range(STEP):
                    piece = field_buf[h, row + r, :, b * LANES:(b + 1) * LANES].astype(F32)
                    pieces.append((piece * scale[:, r:r + 1]).astype(BF16))
                columns.append(jnp.concatenate(pieces, axis=0))
            dequant = jnp.concatenate(columns, axis=1)
            result = dot(dequant, weight_buf[h]).reshape(STEP, half, LANES)
            if h == 0:
                coef[pl.ds(row, STEP)] = result
            else:
                coef[pl.ds(row, STEP)] += result

    project(0, 0, steps)

    first = coef[:, 0, :]
    second = coef[:, 1, :]
    both = first + pltpu.roll(second, modes, 1)
    owners = ab_part.shape[0]
    chunk = rows // owners
    ab_part[...] = both.reshape(owners, chunk, LANES)
    pl.semaphore_wait(barrier, cells_n - 1 + groups - 1)

    def ab_copy(owner, source):
        return pltpu.make_async_remote_copy(
            src_ref=ab_part.at[owner], dst_ref=ab_recv.at[source],
            send_sem=ab_send.at[owner], recv_sem=ab_sem.at[source],
            device_id={"cell": owner}, device_id_type=MESH,
        )

    def abf_copy(owner, target):
        return pltpu.make_async_remote_copy(
            src_ref=ab_full.at[owner], dst_ref=ab_full.at[owner],
            send_sem=abf_send.at[target], recv_sem=abf_sem.at[owner],
            device_id={"cell": target}, device_id_type=MESH,
        )

    def each(count, me, body):
        def guarded(c):
            @pl.when(c != me)
            def _():
                body(c)
        loop(count, guarded)

    each(owners, cme, lambda o: ab_copy(o, cme).start())

    def as_owner(count, body):
        if count == cells_n:
            body()
        else:
            pl.when(cme < count)(body)

    project(1, 0, steps // 2)

    @functools.partial(as_owner, owners)
    def _():
        ab_full[cme] = ab_part[cme]

        def add(c):
            ab_copy(cme, c).wait_recv()
            ab_full[cme] += ab_recv[c]
        each(cells_n, cme, add)
        each(cells_n, cme, lambda c: abf_copy(cme, c).start())

    project(1, steps // 2, steps)

    each(owners, cme, lambda o: abf_copy(o, cme).wait_recv())
    whole = ab_full[...].reshape(rows, LANES)
    whole_t = whole.T
    a_t, b_t = whole_t[:modes], whole_t[modes:]
    b_split = split(b_t, 0)
    b_left = jnp.concatenate([b_split, b_split], axis=1)
    a_split = split(a_t, 0)

    lane = lax.broadcasted_iota(jnp.int32, (rows, LANES), 1)
    part = ab_part[...].reshape(rows, LANES)
    swapped_part = pltpu.roll(part, modes, 1)
    a_twice = jnp.where(lane < modes, part, swapped_part)
    b_twice = jnp.where(lane < modes, swapped_part, part)
    a_right = jnp.where(lane < modes, 0.0, a_twice)

    sums = jnp.sum(part, axis=0, keepdims=True)
    sums = sums + pltpu.roll(sums, modes, 1)
    own_square = dot(jnp.concatenate([a_split, a_split], axis=1), split(a_twice, 0))
    own_square = own_square[:modes] + own_square[modes:]
    mode_lane = lax.broadcasted_iota(jnp.int32, (modes, LANES), 1)

    core, rank = lax.rem(cme, 2), cme // 2
    mine = pl.ds(core * quarter.shape[0], quarter.shape[0])
    theirs = pl.ds((1 - core) * quarter.shape[0], quarter.shape[0])

    def pair_copy(g):
        return pltpu.make_async_remote_copy(
            src_ref=moment.at[g, theirs], dst_ref=pair_recv.at[g],
            send_sem=pair_send.at[g], recv_sem=pair_sem.at[g],
            device_id={"cell": cme + 1 - 2 * core}, device_id_type=MESH,
        )

    def grp_copy(target, source):
        return pltpu.make_async_remote_copy(
            src_ref=moment.at[target, mine], dst_ref=grp_recv.at[source],
            send_sem=grp_send.at[target], recv_sem=grp_sem.at[source],
            device_id={"grp": target}, device_id_type=MESH,
        )

    pairs = half // groups
    tiles = modes // 8
    for g in range(groups):
        for p in range(0, pairs, 2):
            sides = []
            for s in (g * pairs + p, g * pairs + p + 1):
                sides.append(coef[:, s, :] - (a_right if s < 2 else a_twice))
            product = dot(b_left, split(jnp.concatenate(sides, axis=1), 0))
            product = product[:modes] + product[modes:]
            for q in range(2):
                s = g * pairs + p + q
                matrix = product[:, q * LANES:(q + 1) * LANES]
                if s == 0:
                    matrix = jnp.where(mode_lane < modes, sums, matrix)
                if s == 1:
                    matrix = jnp.where(mode_lane < modes, matrix + own_square, matrix)
                at = (p + q) * tiles
                moment[g, at:at + tiles] = matrix.reshape(tiles, 8, LANES)

        pair_copy(g).start()

    for g in range(groups):
        pair_copy(g).wait_recv()
        moment[g, mine] += pair_recv[g]

        @pl.when(g != gme)
        def _():
            grp_copy(g, gme).start()

    grp_recv[gme] = moment[gme, mine]
    each(groups, gme, lambda g: grp_copy(gme, g).wait_recv())
    total = grp_recv[0]
    for g in range(1, groups):
        total = total + grp_recv[g]
    quarter[...] = total

    cov_owners, share = cov_full.shape[0] // 2, cov_full.shape[1]
    ranks = cells_n // 2
    own = jnp.where(rank < cov_owners, core * cov_owners + rank, -1)

    def cov_copy(owner, source):
        return pltpu.make_async_remote_copy(
            src_ref=quarter.at[pl.ds(owner * share, share)], dst_ref=cell_recv.at[source],
            send_sem=cov_send.at[owner], recv_sem=cov_sem.at[source],
            device_id={"cell": 2 * owner + core}, device_id_type=MESH,
        )

    def covf_copy(owner, target):
        return pltpu.make_async_remote_copy(
            src_ref=cov_full.at[owner], dst_ref=cov_full.at[owner],
            send_sem=covf_send.at[target], recv_sem=covf_sem.at[owner],
            device_id={"cell": target}, device_id_type=MESH,
        )

    each(cov_owners, rank, lambda o: cov_copy(o, rank).start())

    def as_cov_owner(body):
        if cov_owners == ranks:
            body()
        else:
            pl.when(rank < cov_owners)(body)

    @as_cov_owner
    def _():
        place = core * cov_owners + rank
        cov_full[place] = quarter[pl.ds(rank * share, share)]

        def add(c):
            cov_copy(rank, c).wait_recv()
            cov_full[place] += cell_recv[c]
        each(ranks, rank, add)
        each(cells_n, cme, lambda c: covf_copy(place, c).start())

    slots = 2 * half
    count = order_ref.shape[1]
    param = lax.broadcasted_iota(jnp.int32, (slots, count), 0)
    chosen = (order_ref[...] == param).astype(F32).astype(BF16)
    swap = lax.broadcasted_iota(jnp.int32, (count, slots), 0) + 2
    place = lax.broadcasted_iota(jnp.int32, (count, slots), 1)
    per = 2 * pairs
    stands = (lax.rem(place, per) // pairs) * half + (place // per) * pairs + lax.rem(place, pairs)
    select = dot(chosen, (stands == swap).astype(F32).astype(BF16))
    out_row = lax.broadcasted_iota(jnp.int32, (slots, slots), 0)
    in_row = lax.broadcasted_iota(jnp.int32, (slots, slots), 1)
    select = jnp.where((out_row == count) & (in_row == 1), 1.0, select).astype(BF16)
    select = jnp.concatenate([select] * 4, axis=1)
    basis_four = jnp.concatenate([phi_t] * 4, axis=0)

    each(2 * cov_owners, own, lambda o: covf_copy(o, cme).wait_recv())
    pair_rows = cov_full[...].reshape(pairs * modes, LANES)
    matrices = [pair_rows[p * modes:(p + 1) * modes] * (1.0 / row_total) for p in range(pairs)]
    average = matrices[0] * 0.5
    outer = average * jnp.pad(average.T[:modes], ((0, 0), (0, LANES - modes)))
    special = (mode_lane < modes) & (gme == 0)
    matrices[1] = jnp.where(special, matrices[1] * 0.5 - outer, matrices[1])
    left = jnp.concatenate(
        [jnp.where(mode_lane < modes, m, 0.0) for m in matrices]
        + [jnp.where(mode_lane < modes, 0.0, m) for m in matrices],
        axis=0,
    )
    products = dot(split(left, 1), basis_four)
    cells = products.shape[1]
    products = products.reshape(per, modes, cells) * phi[None]
    map_recv[gme] = jnp.sum(products, axis=1) * cell_total

    def map_copy(source, target):
        return pltpu.make_async_remote_copy(
            src_ref=map_recv.at[source], dst_ref=map_recv.at[source],
            send_sem=map_send.at[target], recv_sem=map_sem.at[source],
            device_id={"grp": target}, device_id_type=MESH,
        )

    each(groups, gme, lambda g: map_copy(gme, g).start())
    each(groups, gme, lambda g: map_copy(g, gme).wait_recv())
    maps = map_recv[...].reshape(slots, cells)
    high = maps.astype(BF16)
    rest = maps - high.astype(F32)
    middle = rest.astype(BF16)
    low = (rest - middle.astype(F32)).astype(BF16)
    parts = jnp.concatenate([high, middle, low, jnp.zeros_like(low)], axis=0)
    out_ref[...] = dot(select, parts)

    each(owners, cme, lambda o: ab_copy(o, cme).wait_send())
    each(groups, gme, lambda g: grp_copy(g, gme).wait_send())
    each(cov_owners, rank, lambda o: cov_copy(o, rank).wait_send())
    for g in range(groups):
        pair_copy(g).wait_send()
    each(groups, gme, lambda g: map_copy(gme, g).wait_send())
    as_owner(owners, lambda: each(cells_n, cme, lambda c: abf_copy(cme, c).wait_send()))
    as_cov_owner(lambda: each(
        cells_n, cme, lambda c: covf_copy(core * cov_owners + rank, c).wait_send()
    ))


def on_device(fields, scales, pod_basis, param_order):
    groups = lax.axis_size("grp")
    cells_n = lax.axis_size("cell")
    rows, slots, cells = fields.shape
    blocks = scales.shape[2]
    modes = pod_basis.shape[1]
    half = slots // 2
    pairs = half // groups
    count = param_order.shape[0]
    owners = min(cells_n, rows // 8)
    tiles = pairs * modes // 8
    kept = tiles // 2
    cov_owners = min(cells_n // 2, kept)
    share = kept // cov_owners
    dma = pltpu.SemaphoreType.DMA
    anywhere = pl.BlockSpec(memory_space=pl.ANY)
    vmem = pl.BlockSpec(memory_space=pltpu.VMEM)
    packed = pl.pallas_call(
        functools.partial(
            kernel, groups, cells_n, float(rows * groups), float(cells * cells_n)
        ),
        out_shape=jax.ShapeDtypeStruct((slots, cells), F32),
        in_specs=[anywhere] * 4,
        out_specs=vmem,
        scratch_shapes=[
            pltpu.VMEM((slots, blocks, rows), F32),
            pltpu.VMEM((modes, cells), BF16),
            pltpu.VMEM((1, count), jnp.int32),
            pltpu.VMEM((2, rows, half, cells), BF16),
            pltpu.VMEM((blocks, slots, rows), F32),
            pltpu.VMEM((2, cells, LANES), BF16),
            pltpu.VMEM((rows, half, LANES), F32),
            pltpu.VMEM((owners, rows // owners, LANES), F32),
            pltpu.VMEM((cells_n, rows // owners, LANES), F32),
            pltpu.VMEM((owners, rows // owners, LANES), F32),
            pltpu.VMEM((groups, tiles, 8, LANES), F32),
            pltpu.VMEM((groups, kept, 8, LANES), F32),
            pltpu.VMEM((groups, kept, 8, LANES), F32),
            pltpu.VMEM((kept, 8, LANES), F32),
            pltpu.VMEM((cells_n // 2, share, 8, LANES), F32),
            pltpu.VMEM((2 * cov_owners, share, 8, LANES), F32),
            pltpu.VMEM((groups, 2 * pairs, cells), F32),
            dma((3,)), dma((2, rows // STEP)),
            dma((owners,)), dma((cells_n,)), dma((cells_n,)), dma((owners,)),
            dma((groups,)), dma((groups,)), dma((groups,)), dma((groups,)),
            dma((cov_owners,)), dma((cells_n // 2,)), dma((cells_n,)), dma((2 * cov_owners,)),
            dma((groups,)), dma((groups,)),
        ],
        compiler_params=pltpu.CompilerParams(
            collective_id=0, has_side_effects=True, vmem_limit_bytes=62 * 2**20
        ),
        cost_estimate=pl.CostEstimate(
            flops=2 * rows * slots * cells * modes, bytes_accessed=2 * rows * slots * cells,
            transcendentals=0,
        ),
    )(
        fields,
        jnp.transpose(scales, (1, 2, 0)),
        jnp.transpose(pod_basis),
        param_order.reshape(1, count),
    )
    return packed[:count], packed[count]


def solution(mesh):
    placed = (P("grp", None, "cell"), P("grp", None, "cell"), P("cell", None), P())
    return jax.shard_map(
        on_device,
        mesh=mesh,
        in_specs=placed,
        out_specs=(P(None, "cell"), P("cell")),
        check_vma=False,
    )
```
